256 devices in a mesh: qa: 8 (over y_lo, x), qb: 32 (over y_hi, z, core).
Axes of the slice: x: 4, y: 4 (y_hi: 2, y_lo: 2; y = y_hi * 2 + y_lo), z: 8, core: 2. Of those that a mesh axis runs over, the one named last changes fastest.
Arguments:
- amplitudes: float32 [2, 16777216], P(None, ('qa', 'qb')), may hold values from -6 to 6
- gate_blocks: float32 [4, 6, 2, 128, 128], replicated, may hold values from -0.375 to 0.375
- phase_low: float32 [4, 256], replicated, may hold values from -3.140625 to 3.140625
- phase_high: float32 [4, 256], replicated, may hold values from -3.140625 to 3.140625
- phase_global: float32 [4, 8, 32], P(None, 'qa', 'qb'), may hold values from -3.140625 to 3.140625
Outputs:
- final_state: float32 [2, 16777216], P(None, ('qa', 'qb'))
The draws below stay inside these ranges and needn't reach their ends.
All inputs are finite; a program needn't handle non-finite values.
Results may differ from the reference program's by a relative error of at most 0.00011.
Values sent between devices are 32-bit elements; how exact they have to be, the bound alone decides.
A program may use at most 64 MiB of HBM per device.

```python
import jax
import jax.numpy as jnp
from jax import lax

GQ = 7
SEG = 4
GATES = 6
LOWQ = 8
HIGHQ = 8
AMPS = 16777216
N_QA = 8
N_QB = 32


def shard_levels(stream_key, shape, shards, smallest, largest):
    gain, own = 1.0, jax.random.fold_in(stream_key, 6)
    for axis_at, blocks in shards:
        heights = jnp.exp(jax.random.uniform(jax.random.fold_in(own, axis_at), (blocks,), jnp.float32, smallest / len(shards), largest / len(shards)))
        gain = gain * jnp.repeat(heights, shape[axis_at] // blocks).reshape([-1 if axis == axis_at else 1 for axis in range(len(shape))])
    return gain


def normal_values(own_key, dims, scale, reach, split=(), kind=jnp.bfloat16):
    loudness = shard_levels(own_key, dims, split, -0.22, 0.18) if split else 1.0
    entries = jax.random.normal(own_key, dims, jnp.float32) * scale * loudness
    return jnp.minimum(jnp.maximum(entries, -reach), reach).astype(kind)


def setup_inputs(seed: int = 0) -> dict:
    keys = jax.random.split(jax.random.key(seed), 6)
    amplitudes = normal_values(keys[0], (2, AMPS), 1.0, 6.0, ((1, 256),), jnp.float32)
    gate_blocks = normal_values(keys[1], (SEG, GATES, 2, 2 ** GQ, 2 ** GQ), (2 * 2 ** GQ) ** -0.5, 0.375, (), jnp.float32)
    phase_low = jnp.clip(jax.random.uniform(keys[2], (SEG, 2 ** LOWQ), jnp.float32, -3.140625, 3.140625), -3.140625, 3.140625)
    phase_high = jnp.clip(jax.random.uniform(keys[3], (SEG, 2 ** HIGHQ), jnp.float32, -3.140625, 3.140625), -3.140625, 3.140625)
    phase_global = jnp.clip(jax.random.uniform(keys[4], (SEG, N_QA, N_QB), jnp.float32, -3.140625, 3.140625), -3.140625, 3.140625)
    return dict(amplitudes=amplitudes, gate_blocks=gate_blocks, phase_low=phase_low, phase_high=phase_high, phase_global=phase_global)


def gate_part(values, matrix, where):
    if where == 0:
        return jnp.einsum("brj,kj->brk", values, matrix, precision=lax.Precision.HIGHEST)
    if where == 1:
        return jnp.einsum("bhjl,kj->bhkl", values, matrix, precision=lax.Precision.HIGHEST)
    return jnp.einsum("kj,bjr->bkr", matrix, values, precision=lax.Precision.HIGHEST)


def apply_gate(state, matrix, where):
    width = matrix.shape[-1]
    blocks, cells = state.shape[1], state.shape[2]
    if where == 0:
        shape = (blocks, cells // width, width)
    elif where == 1:
        shape = (blocks, cells // (width * width), width, width)
    else:
        shape = (blocks, width, cells // width)
    real = state[0].reshape(shape)
    imag = state[1].reshape(shape)
    out_real = gate_part(real, matrix[0], where) - gate_part(imag, matrix[1], where)
    out_imag = gate_part(real, matrix[1], where) + gate_part(imag, matrix[0], where)
    return jnp.stack([out_real.reshape(blocks, cells), out_imag.reshape(blocks, cells)])


def apply_phase(state, low_angles, high_angles, global_angles):
    local = (high_angles[:, None] + low_angles[None, :]).reshape(-1)
    theta = global_angles.reshape(-1, 1) + local[None, :]
    cosine = jnp.cos(theta)
    sine = jnp.sin(theta)
    return jnp.stack([state[0] * cosine - state[1] * sine, state[0] * sine + state[1] * cosine])


def reference(amplitudes, gate_blocks, phase_low, phase_high, phase_global):
    cells = amplitudes.shape[1] // (N_QA * N_QB)
    state = amplitudes.reshape(2, N_QA * N_QB, cells)
    for segment in range(SEG):
        for gate in range(GATES):
            state = apply_gate(state, gate_blocks[segment, gate], gate % 3)
        state = apply_phase(state, phase_low[segment], phase_high[segment], phase_global[segment])
        if segment == 0 or segment == 2:
            grid = state.reshape(2, N_QA, N_QB, N_QA, cells // N_QA)
            state = jnp.transpose(grid, (0, 3, 2, 1, 4)).reshape(2, N_QA * N_QB, cells)
        elif segment == 1:
            grid = state.reshape(2, N_QA, N_QB, N_QB, cells // N_QB)
            state = jnp.transpose(grid, (0, 1, 3, 2, 4)).reshape(2, N_QA * N_QB, cells)
    return state.reshape(2, N_QA * N_QB * cells)
```

```python
import jax
import jax.numpy as jnp
from jax import lax
from jax.experimental import pallas as pl
from jax.experimental.pallas import tpu as pltpu
from jax.sharding import PartitionSpec as P

F32, BF16 = jnp.float32, jnp.bfloat16
MESH = pl.DeviceIdType.MESH


def dot(a, b):
    return lax.dot_general(a, b, (((1,), (0,)), ((), ())), preferred_element_type=F32)


def dot_t(a, b):
    return lax.dot_general(a, b, (((1,), (1,)), ((), ())), preferred_element_type=F32)


def parts(x):
    high = x.astype(BF16)
    return high, (x - high.astype(F32)).astype(BF16)


def dot3(wh, wl, x):
    xh, xl = parts(x)
    return dot(wh, xh) + dot(wh, xl) + dot(wl, xh)


def iota(shape, axis):
    return lax.broadcasted_iota(jnp.int32, shape, axis)


def half_swap(x, y):
    low = iota(x.shape, 1) < 64
    xr, yr = pltpu.roll(x, 64, 1), pltpu.roll(y, 64, 1)
    return jnp.where(low, x, yr), jnp.where(low, xr, y)


def other_part(x):
    tiles = x.reshape(x.shape[0] // 8, 8, x.shape[1])
    return pltpu.roll(tiles, 4, 1).reshape(x.shape)


def part_sign(shape):
    return jnp.where((iota(shape, 0) // 4) % 2 == 0, -1.0, 1.0).astype(F32)


def embed(re, im):
    return jnp.concatenate(
        [jnp.concatenate([re, -im], axis=1), jnp.concatenate([im, re], axis=1)], axis=0
    )


def kernel(
    amp, gates, p_low, p_high, p_glob, out,
    amp_v, gates_v, low_v, high_v, glob_s, order, wh, wl, bh, bl, full, sends, recvs,
    row_t, mid_t, last_t, in_sem, gate_sem, send_sem, recv_sem,
):
    qa, qb = lax.axis_index("qa"), lax.axis_index("qb")

    gate_copies = [
        pltpu.make_async_copy(
            gates.at[pl.ds(12 * s, 12)], gates_v.at[pl.ds(12 * s, 12)], gate_sem.at[s]
        )
        for s in range(4)
    ]
    amp_copy = pltpu.make_async_copy(amp, amp_v, in_sem.at[0])
    small = [
        pltpu.make_async_copy(p_low, low_v, in_sem.at[1]),
        pltpu.make_async_copy(p_high, high_v, in_sem.at[2]),
        pltpu.make_async_copy(p_glob, glob_s, in_sem.at[3]),
    ]
    gate_copies[0].start()
    amp_copy.start()
    for copy in small:
        copy.start()
    for s in range(1, 4):
        gate_copies[s].start()

    barrier = pltpu.get_barrier_semaphore()

    def greet(axis, me, count):
        def step(i, carry):
            peer = lax.rem(me + i, count)
            pl.semaphore_signal(barrier, inc=1, device_id={axis: peer}, device_id_type=MESH)
            return carry

        lax.fori_loop(1, count, step, 0)

    greet("qa", qa, 8)
    greet("qb", qb, 32)

    p, n = iota((256, 256), 0), iota((256, 256), 1)
    at0 = ((p // 4) % 2) * 128 + ((p // 16) % 8) * 16 + (p % 4) * 4 + ((p // 8) % 2) * 2 + p // 128
    at1 = ((p // 4) % 2) * 128 + (p // 8) * 4 + p % 4
    at2 = (p % 2) * 128 + p // 2
    for i, at in enumerate((at0, at1, at2)):
        order[i] = jnp.where(n == at, 1.0, 0.0).astype(BF16)

    def real_gate(s, g):
        at = (s * 6 + g) * 2
        return embed(gates_v[at], gates_v[at + 1])

    def prepare(s, i, rows, cols):
        h, l = parts(real_gate(s, 1 + i + i // 2))
        if rows is not None:
            both = dot(order[rows], jnp.concatenate([h, l], axis=1)).astype(BF16)
            h, l = both[:, :256], both[:, 256:]
        wh[4 * s + i] = dot_t(h, order[cols]).astype(BF16)
        wl[4 * s + i] = dot_t(l, order[cols]).astype(BF16)

    def prepare_range(s, first, last):
        def step(i, carry):
            prepare(s, i, i % 2, i % 2)
            return carry

        lax.fori_loop(first, last, step, 0)

    def joined_low(s):
        a, b = (s * 6 + 3) * 2, s * 12
        ah, al = parts(embed(gates_v[a], gates_v[a + 1]))
        return dot3(ah, al, jnp.concatenate([gates_v[b], gates_v[b + 1]], axis=0))

    def prepare_low(slot, s, low_cos, low_sin):
        first, second = joined_low(s), joined_low(s + 1)
        re, im = second[:128], second[128:]
        for b7 in range(2):
            co = low_cos[s : s + 1, 128 * b7 : 128 * b7 + 128]
            si = low_sin[s : s + 1, 128 * b7 : 128 * b7 + 128]
            ah, al = parts(embed(re * co - im * si, re * si + im * co))
            h, l = parts(dot3(ah, al, first))
            bh[slot, b7] = jnp.concatenate([h, h], axis=1)
            bl[slot, b7] = l

    def apply_low(slot, b7, x):
        xh, xl = parts(x)
        y = dot_t(jnp.concatenate([xh, xl], axis=1), bh[slot, b7]) + dot_t(xh, bl[slot, b7])
        return y[:, :128] + part_sign((512, 128)) * other_part(y[:, 128:])

    def expand(one_hot, co, si):
        lanes = jnp.concatenate(
            [jnp.broadcast_to(co, (128, 256)), jnp.broadcast_to(si, (128, 256))], axis=0
        )
        h, l = parts(lanes)
        both = dot_t(one_hot, h) + dot_t(one_hot, l)
        return both[:, :128], both[:, 128:]

    def row_one_hot():
        r, c = iota((512, 256), 0), iota((512, 256), 1)
        at = ((r // 16) * 4 + r % 4) * 2 + (r // 8) % 2
        return jnp.where(c == at, 1.0, 0.0).astype(BF16)

    def turn(x, table, at):
        return x * table[at, 0] + other_part(x) * table[at, 1]

    def full_middle(w, src):
        x = jnp.concatenate(
            [
                jnp.concatenate([src[b7, u * 128 : u * 128 + 128] for b7 in range(2)], axis=0)
                for u in range(4)
            ],
            axis=1,
        )
        y = dot3(wh[w], wl[w], x)
        for u in range(4):
            for b7 in range(2):
                full[b7, u * 128 : u * 128 + 128] = y[
                    128 * b7 : 128 * b7 + 128, 128 * u : 128 * u + 128
                ]

    def columns(x):
        x = x.reshape(32, 2, 8, 128)
        return jnp.concatenate([x[:, b8].reshape(256, 128) for b8 in range(2)], axis=1)

    def rows_again(y):
        halves = [y[:, 128 * b8 : 128 * b8 + 128].reshape(32, 1, 8, 128) for b8 in range(2)]
        return jnp.concatenate(halves, axis=1).reshape(512, 128)

    def top_gate(w, x):
        return rows_again(dot3(wh[w], wl[w], columns(x)))

    def full_top(w):
        x = jnp.concatenate([columns(full[b7]) for b7 in range(2)], axis=1)
        y = dot3(wh[w], wl[w], x)
        for b7 in range(2):
            full[b7] = rows_again(y[:, 256 * b7 : 256 * b7 + 256])

    def middle_gate(w, x):
        a, b = half_swap(x[:256], x[256:])
        x = jnp.concatenate(
            [
                jnp.concatenate([a[128 * u : 128 * u + 128], b[128 * u : 128 * u + 128]], axis=0)
                for u in range(2)
            ],
            axis=1,
        )
        y = dot3(wh[w], wl[w], x)
        a = jnp.concatenate([y[:128, :128], y[:128, 128:]], axis=0)
        b = jnp.concatenate([y[128:, :128], y[128:, 128:]], axis=0)
        return jnp.concatenate(half_swap(a, b), axis=0)

    def start(stage, k, axis, me, count):
        size = 512 // count

        def step(i, carry):
            peer = lax.rem(me + i, count)
            pltpu.make_async_remote_copy(
                src_ref=sends.at[stage, k, pl.ds(pl.multiple_of(peer * size, size), size)],
                dst_ref=recvs.at[stage, k, pl.ds(pl.multiple_of(me * size, size), size)],
                send_sem=send_sem.at[stage, k],
                recv_sem=recv_sem.at[stage, k],
                device_id={axis: peer},
                device_id_type=MESH,
            ).start()
            return carry

        lax.fori_loop(1, count, step, 0)
        own = pl.ds(pl.multiple_of(me * size, size), size)
        recvs[stage, k, own, :] = sends[stage, k, own, :]

    def finish(bufs, sem, stage, k, count):
        moved = 512 - 512 // count
        view = bufs.at[stage, k, pl.ds(0, moved)]
        pltpu.make_async_copy(view, view, sem.at[stage, k]).wait()

    gate_copies[0].wait()
    prepare(0, 0, 0, 2)
    prepare_range(0, 1, 4)
    amp_copy.wait()
    x = jnp.concatenate([amp_v[256 * u : 256 * u + 256, :] for u in range(4)], axis=1)
    y = dot3(wh[0], wl[0], x)
    for u in range(4):
        for b7 in range(2):
            full[b7, u * 128 : u * 128 + 128] = y[
                128 * b7 : 128 * b7 + 128, 128 * u : 128 * u + 128
            ]
    full_top(1)
    full_middle(2, full)

    for copy in small:
        copy.wait()
    low_cos, low_sin = jnp.cos(low_v[...]), jnp.sin(low_v[...])
    seg = iota((4, 256), 0)
    glob = jnp.zeros((4, 256), F32)
    for s in range(4):
        glob = jnp.where(seg == s, glob_s[s, 0, 0], glob)
    row_cos, row_sin = jnp.cos(high_v[...] + glob), jnp.sin(high_v[...] + glob)

    def row_table(s):
        c, t = expand(row_one_hot(), row_cos[s : s + 1], row_sin[s : s + 1])
        row_t[s, 0] = c
        row_t[s, 1] = part_sign((512, 128)) * t

    row_table(0)
    gate_copies[1].wait()
    prepare_low(0, 0, low_cos, low_sin)
    a, b = half_swap(apply_low(0, 0, full[0]), apply_low(0, 1, full[1]))
    full[0] = a
    full[1] = b
    pl.semaphore_wait(barrier, 38)

    def leave0(k, carry):
        sends[0, k] = turn(top_gate(3, full[k]), row_t, 0)
        start(0, k, "qa", qa, 8)
        return carry

    lax.fori_loop(0, 2, leave0, 0)

    prepare_range(1, 0, 4)
    row_table(1)
    v, w = half_swap(
        jnp.broadcast_to(low_cos[1:2, :128], (8, 128)), jnp.broadcast_to(low_cos[1:2, 128:], (8, 128))
    )
    vs, ws = half_swap(
        jnp.broadcast_to(low_sin[1:2, :128], (8, 128)), jnp.broadcast_to(low_sin[1:2, 128:], (8, 128))
    )
    for k, (co, si) in enumerate(((v, vs), (w, ws))):
        co, si = co[:1], si[:1]
        sign = part_sign((512, 128))
        mid_t[k, 0] = row_t[1, 0] * co - row_t[1, 1] * sign * si
        mid_t[k, 1] = row_t[1, 1] * co + row_t[1, 0] * sign * si

    def between(k, carry):
        finish(recvs, recv_sem, 0, k, 8)
        x = middle_gate(4, recvs[0, k])
        x = top_gate(5, x)
        x = middle_gate(6, x)
        x = top_gate(7, x)
        sends[1, k] = turn(x, mid_t, k)
        start(1, k, "qb", qb, 32)
        return carry

    lax.fori_loop(0, 2, between, 0)

    gate_copies[2].wait()
    gate_copies[3].wait()
    prepare_range(2, 0, 4)
    prepare_range(3, 0, 3)
    prepare(3, 3, None, 1)
    prepare_low(1, 2, low_cos, low_sin)
    row_table(2)
    r, c = iota((256, 256), 0), iota((256, 256), 1)
    one_hot = jnp.where(c == (r % 128) * 2 + r // 128, 1.0, 0.0).astype(BF16)
    co3, si3 = expand(one_hot, row_cos[3:4], row_sin[3:4])
    for b8 in range(2):
        rc, rs = co3[128 * b8 : 128 * b8 + 128], si3[128 * b8 : 128 * b8 + 128]
        for b7 in range(2):
            lc = low_cos[3:4, 128 * b7 : 128 * b7 + 128]
            ls = low_sin[3:4, 128 * b7 : 128 * b7 + 128]
            last_t[b8, b7, 0] = rc * lc - rs * ls
            last_t[b8, b7, 1] = rs * lc + rc * ls

    def arrive1(k, carry):
        finish(recvs, recv_sem, 1, k, 32)
        x = middle_gate(8, recvs[1, k])
        x = top_gate(9, x)
        full[k] = middle_gate(10, x)
        return carry

    lax.fori_loop(0, 2, arrive1, 0)
    a, b = half_swap(full[0], full[1])
    full[0] = a
    full[1] = b

    def leave2(b7, carry):
        x = apply_low(1, b7, full[b7])
        sends[2, b7] = turn(top_gate(11, x), row_t, 2)
        start(2, b7, "qa", qa, 8)
        return carry

    lax.fori_loop(0, 2, leave2, 0)

    for b7 in range(2):
        finish(recvs, recv_sem, 2, b7, 8)
    full_middle(12, recvs.at[2])
    full_top(13)
    full_middle(14, full)
    for b7 in range(2):
        y = dot3(wh[15], wl[15], columns(full[b7]))
        for b8 in range(2):
            re = y[:128, 128 * b8 : 128 * b8 + 128]
            im = y[128:, 128 * b8 : 128 * b8 + 128]
            co, si = last_t[b8, b7, 0], last_t[b8, b7, 1]
            at = 4 * b8 + 2 * b7
            out[pl.ds(at, 128, stride=8), :] = re * co - im * si
            out[pl.ds(at + 1, 128, stride=8), :] = im * co + re * si

    for stage, count in ((0, 8), (1, 32), (2, 8)):
        for k in range(2):
            finish(sends, send_sem, stage, k, count)


def body(amplitudes, gate_blocks, phase_low, phase_high, phase_global):
    cells = amplitudes.shape[1]
    rows = cells // 128
    amp = amplitudes.reshape(2, rows, 128).transpose(1, 0, 2).reshape(2 * rows, 128)
    anywhere = pl.BlockSpec(memory_space=pl.ANY)
    result = pl.pallas_call(
        kernel,
        name="circuit",
        out_shape=jax.ShapeDtypeStruct((2 * rows, 128), F32),
        in_specs=[anywhere] * 5,
        out_specs=pl.BlockSpec(memory_space=pltpu.VMEM),
        scratch_shapes=[
            pltpu.VMEM((1024, 128), F32),
            pltpu.VMEM((48, 128, 128), F32),
            pltpu.VMEM((4, 256), F32),
            pltpu.VMEM((4, 256), F32),
            pltpu.SMEM((4, 1, 1), F32),
            pltpu.VMEM((3, 256, 256), BF16),
            pltpu.VMEM((16, 256, 256), BF16),
            pltpu.VMEM((16, 256, 256), BF16),
            pltpu.VMEM((2, 2, 256, 256), BF16),
            pltpu.VMEM((2, 2, 256, 128), BF16),
            pltpu.VMEM((2, 512, 128), F32),
            pltpu.VMEM((3, 2, 512, 128), F32),
            pltpu.VMEM((3, 2, 512, 128), F32),
            pltpu.VMEM((3, 2, 512, 128), F32),
            pltpu.VMEM((2, 2, 512, 128), F32),
            pltpu.VMEM((2, 2, 2, 128, 128), F32),
            pltpu.SemaphoreType.DMA((4,)),
            pltpu.SemaphoreType.DMA((4,)),
            pltpu.SemaphoreType.DMA((3, 2)),
            pltpu.SemaphoreType.DMA((3, 2)),
        ],
        compiler_params=pltpu.CompilerParams(
            collective_id=0, has_side_effects=True, vmem_limit_bytes=40 << 20
        ),
    )(amp, gate_blocks.reshape(48, 128, 128), phase_low, phase_high, phase_global)
    return result.reshape(rows, 2, 128).transpose(1, 0, 2).reshape(2, cells)


def solution(mesh):
    return jax.shard_map(
        body,
        mesh=mesh,
        in_specs=(P(None, ("qa", "qb")), P(), P(), P(), P(None, "qa", "qb")),
        out_specs=P(None, ("qa", "qb")),
        check_vma=False,
    )
```

```python
import jax
import jax.numpy as jnp
from jax import lax
from jax.experimental import pallas as pl
from jax.experimental.pallas import tpu as pltpu
from jax.sharding import PartitionSpec as P

F32, BF16 = jnp.float32, jnp.bfloat16
MESH = pl.DeviceIdType.MESH


def dot(a, b):
    return lax.dot_general(a, b, (((1,), (0,)), ((), ())), preferred_element_type=F32)


def dot_t(a, b):
    return lax.dot_general(a, b, (((1,), (1,)), ((), ())), preferred_element_type=F32)


def parts(x):
    high = x.astype(BF16)
    return high, (x - high.astype(F32)).astype(BF16)


def dot3(wh, wl, x):
    xh, xl = parts(x)
    return dot(wh, xh) + dot(wh, xl) + dot(wl, xh)


def iota(shape, axis):
    return lax.broadcasted_iota(jnp.int32, shape, axis)


def half_swap(x, y):
    low = iota(x.shape, 1) < 64
    xr, yr = pltpu.roll(x, 64, 1), pltpu.roll(y, 64, 1)
    return jnp.where(low, x, yr), jnp.where(low, xr, y)


def other_part(x):
    tiles = x.reshape(x.shape[0] // 8, 8, x.shape[1])
    return pltpu.roll(tiles, 4, 1).reshape(x.shape)


def part_sign(shape):
    return jnp.where((iota(shape, 0) // 4) % 2 == 0, -1.0, 1.0).astype(F32)


def embed(re, im):
    return jnp.concatenate(
        [jnp.concatenate([re, -im], axis=1), jnp.concatenate([im, re], axis=1)], axis=0
    )


def kernel(
    amp, gates, p_low, p_high, p_glob, out,
    amp_v, gates_v, low_v, high_v, glob_s, order, wh, wl, bh, bl, full, sends, recvs,
    row_t, mid_t, last_t, in_sem, gate_sem, send_sem, recv_sem,
):
    qa, qb = lax.axis_index("qa"), lax.axis_index("qb")

    gate_copies = [
        pltpu.make_async_copy(
            gates.at[pl.ds(12 * s, 12)], gates_v.at[pl.ds(12 * s, 12)], gate_sem.at[s]
        )
        for s in range(4)
    ]
    amp_copy = pltpu.make_async_copy(amp, amp_v, in_sem.at[0])
    small = [
        pltpu.make_async_copy(p_low, low_v, in_sem.at[1]),
        pltpu.make_async_copy(p_high, high_v, in_sem.at[2]),
        pltpu.make_async_copy(p_glob, glob_s, in_sem.at[3]),
    ]
    gate_copies[0].start()
    amp_copy.start()
    for copy in small:
        copy.start()
    gate_copies[1].start()

    barrier = pltpu.get_barrier_semaphore()

    def greet(axis, me, count):
        def step(i, carry):
            peer = lax.rem(me + i, count)
            pl.semaphore_signal(barrier, inc=1, device_id={axis: peer}, device_id_type=MESH)
            return carry

        lax.fori_loop(1, count, step, 0)

    greet("qa", qa, 8)
    greet("qb", qb, 32)

    p, n = iota((256, 256), 0), iota((256, 256), 1)
    at0 = ((p // 4) % 2) * 128 + ((p // 16) % 8) * 16 + (p % 4) * 4 + ((p // 8) % 2) * 2 + p // 128
    at1 = ((p // 4) % 2) * 128 + (p // 8) * 4 + p % 4
    at2 = (p % 2) * 128 + p // 2
    for i, at in enumerate((at0, at1, at2)):
        order[i] = jnp.where(n == at, 1.0, 0.0).astype(BF16)

    def real_gate(s, g):
        at = (s * 6 + g) * 2
        return embed(gates_v[at], gates_v[at + 1])

    def prepare(s, i, rows, cols):
        h, l = parts(real_gate(s, 1 + i + i // 2))
        if rows is not None:
            both = dot(order[rows], jnp.concatenate([h, l], axis=1)).astype(BF16)
            h, l = both[:, :256], both[:, 256:]
        wh[4 * s + i] = dot_t(h, order[cols]).astype(BF16)
        wl[4 * s + i] = dot_t(l, order[cols]).astype(BF16)

    def prepare_range(s, first, last):
        def step(i, carry):
            prepare(s, i, i % 2, i % 2)
            return carry

        lax.fori_loop(first, last, step, 0)

    def joined_low(s):
        a, b = (s * 6 + 3) * 2, s * 12
        ah, al = parts(embed(gates_v[a], gates_v[a + 1]))
        return dot3(ah, al, jnp.concatenate([gates_v[b], gates_v[b + 1]], axis=0))

    def prepare_low(slot, s, low_cos, low_sin):
        first, second = joined_low(s), joined_low(s + 1)
        re, im = second[:128], second[128:]
        for b7 in range(2):
            co = low_cos[s : s + 1, 128 * b7 : 128 * b7 + 128]
            si = low_sin[s : s + 1, 128 * b7 : 128 * b7 + 128]
            ah, al = parts(embed(re * co - im * si, re * si + im * co))
            h, l = parts(dot3(ah, al, first))
            bh[slot, b7] = jnp.concatenate([h, h], axis=1)
            bl[slot, b7] = l

    def apply_low(slot, b7, x):
        xh, xl = parts(x)
        y = dot_t(jnp.concatenate([xh, xl], axis=1), bh[slot, b7]) + dot_t(xh, bl[slot, b7])
        return y[:, :128] + part_sign((512, 128)) * other_part(y[:, 128:])

    def expand(one_hot, co, si):
        lanes = jnp.concatenate(
            [jnp.broadcast_to(co, (128, 256)), jnp.broadcast_to(si, (128, 256))], axis=0
        )
        h, l = parts(lanes)
        both = dot_t(one_hot, h) + dot_t(one_hot, l)
        return both[:, :128], both[:, 128:]

    def row_one_hot():
        r, c = iota((512, 256), 0), iota((512, 256), 1)
        at = ((r // 16) * 4 + r % 4) * 2 + (r // 8) % 2
        return jnp.where(c == at, 1.0, 0.0).astype(BF16)

    def turn(x, table, at):
        return x * table[at, 0] + other_part(x) * table[at, 1]

    def full_middle(w, src):
        x = jnp.concatenate(
            [
                jnp.concatenate([src[b7, u * 128 : u * 128 + 128] for b7 in range(2)], axis=0)
                for u in range(4)
            ],
            axis=1,
        )
        y = dot3(wh[w], wl[w], x)
        for u in range(4):
            for b7 in range(2):
                full[b7, u * 128 : u * 128 + 128] = y[
                    128 * b7 : 128 * b7 + 128, 128 * u : 128 * u + 128
                ]

    def columns(x):
        x = x.reshape(32, 2, 8, 128)
        return jnp.concatenate([x[:, b8].reshape(256, 128) for b8 in range(2)], axis=1)

    def rows_again(y):
        halves = [y[:, 128 * b8 : 128 * b8 + 128].reshape(32, 1, 8, 128) for b8 in range(2)]
        return jnp.concatenate(halves, axis=1).reshape(512, 128)

    def top_gate(w, x):
        return rows_again(dot3(wh[w], wl[w], columns(x)))

    def full_top(w):
        x = jnp.concatenate([columns(full[b7]) for b7 in range(2)], axis=1)
        y = dot3(wh[w], wl[w], x)
        for b7 in range(2):
            full[b7] = rows_again(y[:, 256 * b7 : 256 * b7 + 256])

    def middle_gate(w, x):
        a, b = half_swap(x[:256], x[256:])
        x = jnp.concatenate(
            [
                jnp.concatenate([a[128 * u : 128 * u + 128], b[128 * u : 128 * u + 128]], axis=0)
                for u in range(2)
            ],
            axis=1,
        )
        y = dot3(wh[w], wl[w], x)
        a = jnp.concatenate([y[:128, :128], y[:128, 128:]], axis=0)
        b = jnp.concatenate([y[128:, :128], y[128:, 128:]], axis=0)
        return jnp.concatenate(half_swap(a, b), axis=0)

    def start(stage, k, axis, me, count):
        size = 512 // count

        def step(i, carry):
            peer = lax.rem(me + i, count)
            pltpu.make_async_remote_copy(
                src_ref=sends.at[stage, k, pl.ds(pl.multiple_of(peer * size, size), size)],
                dst_ref=recvs.at[stage, k, pl.ds(pl.multiple_of(me * size, size), size)],
                send_sem=send_sem.at[stage, k],
                recv_sem=recv_sem.at[stage, k],
                device_id={axis: peer},
                device_id_type=MESH,
            ).start()
            return carry

        lax.fori_loop(1, count, step, 0)
        own = pl.ds(pl.multiple_of(me * size, size), size)
        recvs[stage, k, own, :] = sends[stage, k, own, :]

    def finish(bufs, sem, stage, k, count):
        moved = 512 - 512 // count
        view = bufs.at[stage, k, pl.ds(0, moved)]
        pltpu.make_async_copy(view, view, sem.at[stage, k]).wait()

    for copy in small:
        copy.wait()
    low_cos, low_sin = jnp.cos(low_v[...]), jnp.sin(low_v[...])
    seg = iota((4, 256), 0)
    glob = jnp.zeros((4, 256), F32)
    for s in range(4):
        glob = jnp.where(seg == s, glob_s[0, s], glob)
    row_cos, row_sin = jnp.cos(high_v[...] + glob), jnp.sin(high_v[...] + glob)

    def row_table(s):
        c, t = expand(row_one_hot(), row_cos[s : s + 1], row_sin[s : s + 1])
        row_t[s, 0] = c
        row_t[s, 1] = part_sign((512, 128)) * t

    row_table(0)
    gate_copies[0].wait()
    amp_copy.wait()
    gate_copies[1].wait()
    gate_copies[2].start()
    gate_copies[3].start()
    prepare(0, 0, 0, 2)
    x = jnp.concatenate([amp_v[256 * u : 256 * u + 256, :] for u in range(4)], axis=1)
    y = dot3(wh[0], wl[0], x)
    for u in range(4):
        for b7 in range(2):
            full[b7, u * 128 : u * 128 + 128] = y[
                128 * b7 : 128 * b7 + 128, 128 * u : 128 * u + 128
            ]
    prepare(0, 1, 1, 1)
    full_top(1)
    prepare(0, 2, 0, 0)
    prepare_low(0, 0, low_cos, low_sin)
    full_middle(2, full)
    prepare(0, 3, 1, 1)
    halves = half_swap(apply_low(0, 0, full[0]), apply_low(0, 1, full[1]))
    y = dot3(wh[3], wl[3], jnp.concatenate([columns(h) for h in halves], axis=1))
    for k in range(2):
        sends[0, k] = turn(rows_again(y[:, 256 * k : 256 * k + 256]), row_t, 0)
    pl.semaphore_wait(barrier, 38)
    for k in range(2):
        start(0, k, "qa", qa, 8)

    prepare_range(1, 0, 4)
    row_table(1)
    v, w = half_swap(
        jnp.broadcast_to(low_cos[1:2, :128], (8, 128)), jnp.broadcast_to(low_cos[1:2, 128:], (8, 128))
    )
    vs, ws = half_swap(
        jnp.broadcast_to(low_sin[1:2, :128], (8, 128)), jnp.broadcast_to(low_sin[1:2, 128:], (8, 128))
    )
    for k, (co, si) in enumerate(((v, vs), (w, ws))):
        co, si = co[:1], si[:1]
        sign = part_sign((512, 128))
        mid_t[k, 0] = row_t[1, 0] * co - row_t[1, 1] * sign * si
        mid_t[k, 1] = row_t[1, 1] * co + row_t[1, 0] * sign * si

    def between(k, carry):
        finish(recvs, recv_sem, 0, k, 8)
        x = middle_gate(4, recvs[0, k])
        x = top_gate(5, x)
        x = middle_gate(6, x)
        x = top_gate(7, x)
        sends[1, k] = turn(x, mid_t, k)
        start(1, k, "qb", qb, 32)
        return carry

    lax.fori_loop(0, 2, between, 0)

    gate_copies[2].wait()
    gate_copies[3].wait()
    prepare_range(2, 0, 4)
    prepare_range(3, 0, 3)
    prepare(3, 3, None, 1)
    prepare_low(1, 2, low_cos, low_sin)
    row_table(2)
    r, c = iota((256, 256), 0), iota((256, 256), 1)
    one_hot = jnp.where(c == (r % 128) * 2 + r // 128, 1.0, 0.0).astype(BF16)
    co3, si3 = expand(one_hot, row_cos[3:4], row_sin[3:4])
    for b8 in range(2):
        rc, rs = co3[128 * b8 : 128 * b8 + 128], si3[128 * b8 : 128 * b8 + 128]
        for b7 in range(2):
            lc = low_cos[3:4, 128 * b7 : 128 * b7 + 128]
            ls = low_sin[3:4, 128 * b7 : 128 * b7 + 128]
            last_t[b8, b7, 0] = rc * lc - rs * ls
            last_t[b8, b7, 1] = rs * lc + rc * ls

    def arrive1(k, carry):
        finish(recvs, recv_sem, 1, k, 32)
        x = middle_gate(8, recvs[1, k])
        x = top_gate(9, x)
        full[k] = middle_gate(10, x)
        return carry

    lax.fori_loop(0, 2, arrive1, 0)
    a, b = half_swap(full[0], full[1])
    full[0] = a
    full[1] = b

    def leave2(b7, carry):
        x = apply_low(1, b7, full[b7])
        sends[2, b7] = turn(top_gate(11, x), row_t, 2)
        start(2, b7, "qa", qa, 8)
        return carry

    lax.fori_loop(0, 2, leave2, 0)

    for b7 in range(2):
        finish(recvs, recv_sem, 2, b7, 8)
    full_middle(12, recvs.at[2])
    full_top(13)
    full_middle(14, full)
    for b7 in range(2):
        y = dot3(wh[15], wl[15], columns(full[b7]))
        for b8 in range(2):
            re = y[:128, 128 * b8 : 128 * b8 + 128]
            im = y[128:, 128 * b8 : 128 * b8 + 128]
            co, si = last_t[b8, b7, 0], last_t[b8, b7, 1]
            at = 4 * b8 + 2 * b7
            out[pl.ds(at, 128, stride=8), :] = re * co - im * si
            out[pl.ds(at + 1, 128, stride=8), :] = im * co + re * si

    for stage, count in ((0, 8), (1, 32), (2, 8)):
        for k in range(2):
            finish(sends, send_sem, stage, k, count)


def body(amplitudes, gate_blocks, phase_low, phase_high, phase_global):
    cells = amplitudes.shape[1]
    rows = cells // 128
    amp = amplitudes.reshape(2, rows, 128).transpose(1, 0, 2).reshape(2 * rows, 128)
    anywhere = pl.BlockSpec(memory_space=pl.ANY)
    result = pl.pallas_call(
        kernel,
        name="circuit",
        out_shape=pltpu.VMEM((2 * rows, 128), F32),
        in_specs=[anywhere] * 5,
        out_specs=pl.BlockSpec(memory_space=pltpu.VMEM),
        scratch_shapes=[
            pltpu.VMEM((1024, 128), F32),
            pltpu.VMEM((48, 128, 128), F32),
            pltpu.VMEM((4, 256), F32),
            pltpu.VMEM((4, 256), F32),
            pltpu.SMEM((1, 4), F32),
            pltpu.VMEM((3, 256, 256), BF16),
            pltpu.VMEM((16, 256, 256), BF16),
            pltpu.VMEM((16, 256, 256), BF16),
            pltpu.VMEM((2, 2, 256, 256), BF16),
            pltpu.VMEM((2, 2, 256, 128), BF16),
            pltpu.VMEM((2, 512, 128), F32),
            pltpu.VMEM((3, 2, 512, 128), F32),
            pltpu.VMEM((3, 2, 512, 128), F32),
            pltpu.VMEM((3, 2, 512, 128), F32),
            pltpu.VMEM((2, 2, 512, 128), F32),
            pltpu.VMEM((2, 2, 2, 128, 128), F32),
            pltpu.SemaphoreType.DMA((4,)),
            pltpu.SemaphoreType.DMA((4,)),
            pltpu.SemaphoreType.DMA((3, 2)),
            pltpu.SemaphoreType.DMA((3, 2)),
        ],
        compiler_params=pltpu.CompilerParams(
            collective_id=0, has_side_effects=True, vmem_limit_bytes=60 << 20
        ),
    )(amp, gate_blocks.reshape(48, 128, 128), phase_low, phase_high, phase_global.reshape(1, 4))
    return result.reshape(rows, 2, 128).transpose(1, 0, 2).reshape(2, cells)


def solution(mesh):
    return jax.shard_map(
        body,
        mesh=mesh,
        in_specs=(P(None, ("qa", "qb")), P(), P(), P(), P(None, "qa", "qb")),
        out_specs=P(None, ("qa", "qb")),
        check_vma=False,
    )
```

```python
import jax
import jax.numpy as jnp
from jax import lax
from jax.experimental import pallas as pl
from jax.experimental.pallas import tpu as pltpu
from jax.sharding import PartitionSpec as P

F32, BF16 = jnp.float32, jnp.bfloat16
MESH = pl.DeviceIdType.MESH


def dot(a, b):
    return lax.dot_general(a, b, (((1,), (0,)), ((), ())), preferred_element_type=F32)


def dot_t(a, b):
    return lax.dot_general(a, b, (((1,), (1,)), ((), ())), preferred_element_type=F32)


def parts(x):
    high = x.astype(BF16)
    return high, (x - high.astype(F32)).astype(BF16)


def dot3(wh, wl, x):
    xh, xl = parts(x)
    return dot(wh, xh) + dot(wh, xl) + dot(wl, xh)


def iota(shape, axis):
    return lax.broadcasted_iota(jnp.int32, shape, axis)


def half_swap(x, y):
    low = iota(x.shape, 1) < 64
    xr, yr = pltpu.roll(x, 64, 1), pltpu.roll(y, 64, 1)
    return jnp.where(low, x, yr), jnp.where(low, xr, y)


def other_part(x):
    tiles = x.reshape(x.shape[0] // 8, 8, x.shape[1])
    return pltpu.roll(tiles, 4, 1).reshape(x.shape)


def part_sign(shape):
    return jnp.where((iota(shape, 0) // 4) % 2 == 0, -1.0, 1.0).astype(F32)


def embed(re, im):
    return jnp.concatenate(
        [jnp.concatenate([re, -im], axis=1), jnp.concatenate([im, re], axis=1)], axis=0
    )


def kernel(
    amp, gates, p_low, p_high, p_glob, out,
    amp_v, gates_v, low_v, high_v, glob_s, order, wh, wl, bh, bl, full, sends, recvs,
    row_t, mid_t, last_t, in_sem, gate_sem, send_sem, recv_sem,
):
    qa, qb = lax.axis_index("qa"), lax.axis_index("qb")

    gate_copies = [
        pltpu.make_async_copy(
            gates.at[pl.ds(12 * s, 12)], gates_v.at[pl.ds(12 * s, 12)], gate_sem.at[s]
        )
        for s in range(4)
    ]
    amp_copy = pltpu.make_async_copy(amp, amp_v, in_sem.at[0])
    small = [
        pltpu.make_async_copy(p_low, low_v, in_sem.at[1]),
        pltpu.make_async_copy(p_high, high_v, in_sem.at[2]),
        pltpu.make_async_copy(p_glob, glob_s, in_sem.at[3]),
    ]
    gate_copies[0].start()
    amp_copy.start()
    for copy in small:
        copy.start()
    gate_copies[1].start()

    barrier = pltpu.get_barrier_semaphore()

    def greet(axis, me, count):
        def step(i, carry):
            peer = lax.rem(me + i, count)
            pl.semaphore_signal(barrier, inc=1, device_id={axis: peer}, device_id_type=MESH)
            return carry

        lax.fori_loop(1, count, step, 0)

    greet("qa", qa, 8)
    greet("qb", qb, 32)

    p, n = iota((256, 256), 0), iota((256, 256), 1)
    at0 = ((p // 4) % 2) * 128 + ((p // 16) % 8) * 16 + (p % 4) * 4 + ((p // 8) % 2) * 2 + p // 128
    at1 = ((p // 4) % 2) * 128 + (p // 8) * 4 + p % 4
    at2 = (p % 2) * 128 + p // 2
    for i, at in enumerate((at0, at1, at2)):
        order[i] = jnp.where(n == at, 1.0, 0.0).astype(BF16)

    def real_gate(s, g):
        at = (s * 6 + g) * 2
        return embed(gates_v[at], gates_v[at + 1])

    def prepare(s, i, rows, cols):
        h, l = parts(real_gate(s, 1 + i + i // 2))
        if rows is not None:
            both = dot(order[rows], jnp.concatenate([h, l], axis=1)).astype(BF16)
            h, l = both[:, :256], both[:, 256:]
        wh[4 * s + i] = dot_t(h, order[cols]).astype(BF16)
        wl[4 * s + i] = dot_t(l, order[cols]).astype(BF16)

    def prepare_range(s, first, last):
        def step(i, carry):
            prepare(s, i, i % 2, i % 2)
            return carry

        lax.fori_loop(first, last, step, 0)

    def joined_low(s):
        a, b = (s * 6 + 3) * 2, s * 12
        ah, al = parts(embed(gates_v[a], gates_v[a + 1]))
        return dot3(ah, al, jnp.concatenate([gates_v[b], gates_v[b + 1]], axis=0))

    def prepare_low(slot, s, low_cos, low_sin):
        first, second = joined_low(s), joined_low(s + 1)
        re, im = second[:128], second[128:]
        for b7 in range(2):
            co = low_cos[s : s + 1, 128 * b7 : 128 * b7 + 128]
            si = low_sin[s : s + 1, 128 * b7 : 128 * b7 + 128]
            ah, al = parts(embed(re * co - im * si, re * si + im * co))
            h, l = parts(dot3(ah, al, first))
            bh[slot, b7] = jnp.concatenate([h, h], axis=1)
            bl[slot, b7] = l

    def apply_low(slot, b7, x):
        xh, xl = parts(x)
        y = dot_t(jnp.concatenate([xh, xl], axis=1), bh[slot, b7]) + dot_t(xh, bl[slot, b7])
        return y[:, :128] + part_sign((512, 128)) * other_part(y[:, 128:])

    def expand(one_hot, co, si):
        lanes = jnp.concatenate(
            [jnp.broadcast_to(co, (128, 256)), jnp.broadcast_to(si, (128, 256))], axis=0
        )
        h, l = parts(lanes)
        both = dot_t(one_hot, h) + dot_t(one_hot, l)
        return both[:, :128], both[:, 128:]

    def row_one_hot():
        r, c = iota((512, 256), 0), iota((512, 256), 1)
        at = ((r // 16) * 4 + r % 4) * 2 + (r // 8) % 2
        return jnp.where(c == at, 1.0, 0.0).astype(BF16)

    def turn(x, table, at):
        return x * table[at, 0] + other_part(x) * table[at, 1]

    def full_middle(w, src):
        x = jnp.concatenate(
            [
                jnp.concatenate([src[b7, u * 128 : u * 128 + 128] for b7 in range(2)], axis=0)
                for u in range(4)
            ],
            axis=1,
        )
        y = dot3(wh[w], wl[w], x)
        for u in range(4):
            for b7 in range(2):
                full[b7, u * 128 : u * 128 + 128] = y[
                    128 * b7 : 128 * b7 + 128, 128 * u : 128 * u + 128
                ]

    def columns(x):
        x = x.reshape(32, 2, 8, 128)
        return jnp.concatenate([x[:, b8].reshape(256, 128) for b8 in range(2)], axis=1)

    def rows_again(y):
        halves = [y[:, 128 * b8 : 128 * b8 + 128].reshape(32, 1, 8, 128) for b8 in range(2)]
        return jnp.concatenate(halves, axis=1).reshape(512, 128)

    def top_gate(w, x):
        return rows_again(dot3(wh[w], wl[w], columns(x)))

    def full_top(w):
        x = jnp.concatenate([columns(full[b7]) for b7 in range(2)], axis=1)
        y = dot3(wh[w], wl[w], x)
        for b7 in range(2):
            full[b7] = rows_again(y[:, 256 * b7 : 256 * b7 + 256])

    def middle_gate(w, x):
        a, b = half_swap(x[:256], x[256:])
        x = jnp.concatenate(
            [
                jnp.concatenate([a[128 * u : 128 * u + 128], b[128 * u : 128 * u + 128]], axis=0)
                for u in range(2)
            ],
            axis=1,
        )
        y = dot3(wh[w], wl[w], x)
        a = jnp.concatenate([y[:128, :128], y[:128, 128:]], axis=0)
        b = jnp.concatenate([y[128:, :128], y[128:, 128:]], axis=0)
        return jnp.concatenate(half_swap(a, b), axis=0)

    def start(stage, k, axis, me, count):
        size = 512 // count

        def step(i, carry):
            peer = lax.rem(me + i, count) if axis == "qa" else i - 1 + jnp.where(i > me, 1, 0)
            pltpu.make_async_remote_copy(
                src_ref=sends.at[stage, k, pl.ds(pl.multiple_of(peer * size, size), size)],
                dst_ref=recvs.at[stage, k, pl.ds(pl.multiple_of(me * size, size), size)],
                send_sem=send_sem.at[stage, k],
                recv_sem=recv_sem.at[stage, k],
                device_id={axis: peer},
                device_id_type=MESH,
            ).start()
            return carry

        lax.fori_loop(1, count, step, 0)
        own = pl.ds(pl.multiple_of(me * size, size), size)
        recvs[stage, k, own, :] = sends[stage, k, own, :]

    def finish(bufs, sem, stage, k, count):
        moved = 512 - 512 // count
        view = bufs.at[stage, k, pl.ds(0, moved)]
        pltpu.make_async_copy(view, view, sem.at[stage, k]).wait()

    for copy in small:
        copy.wait()
    low_cos, low_sin = jnp.cos(low_v[...]), jnp.sin(low_v[...])
    seg = iota((4, 256), 0)
    glob = jnp.zeros((4, 256), F32)
    for s in range(4):
        glob = jnp.where(seg == s, glob_s[0, s], glob)
    row_cos, row_sin = jnp.cos(high_v[...] + glob), jnp.sin(high_v[...] + glob)

    def row_table(s):
        c, t = expand(row_one_hot(), row_cos[s : s + 1], row_sin[s : s + 1])
        row_t[s, 0] = c
        row_t[s, 1] = part_sign((512, 128)) * t

    row_table(0)
    gate_copies[0].wait()
    amp_copy.wait()
    gate_copies[1].wait()
    gate_copies[2].start()
    gate_copies[3].start()
    prepare(0, 0, 0, 2)
    x = jnp.concatenate([amp_v[256 * u : 256 * u + 256, :] for u in range(4)], axis=1)
    y = dot3(wh[0], wl[0], x)
    for u in range(4):
        for b7 in range(2):
            full[b7, u * 128 : u * 128 + 128] = y[
                128 * b7 : 128 * b7 + 128, 128 * u : 128 * u + 128
            ]
    prepare(0, 1, 1, 1)
    full_top(1)
    prepare(0, 2, 0, 0)
    prepare_low(0, 0, low_cos, low_sin)
    full_middle(2, full)
    prepare(0, 3, 1, 1)
    halves = half_swap(apply_low(0, 0, full[0]), apply_low(0, 1, full[1]))
    y = dot3(wh[3], wl[3], jnp.concatenate([columns(h) for h in halves], axis=1))
    for k in range(2):
        sends[0, k] = turn(rows_again(y[:, 256 * k : 256 * k + 256]), row_t, 0)
    pl.semaphore_wait(barrier, 38)
    for k in range(2):
        start(0, k, "qa", qa, 8)

    prepare_range(1, 0, 4)
    row_table(1)
    v, w = half_swap(
        jnp.broadcast_to(low_cos[1:2, :128], (8, 128)), jnp.broadcast_to(low_cos[1:2, 128:], (8, 128))
    )
    vs, ws = half_swap(
        jnp.broadcast_to(low_sin[1:2, :128], (8, 128)), jnp.broadcast_to(low_sin[1:2, 128:], (8, 128))
    )
    for k, (co, si) in enumerate(((v, vs), (w, ws))):
        co, si = co[:1], si[:1]
        sign = part_sign((512, 128))
        mid_t[k, 0] = row_t[1, 0] * co - row_t[1, 1] * sign * si
        mid_t[k, 1] = row_t[1, 1] * co + row_t[1, 0] * sign * si

    def between(k, carry):
        finish(recvs, recv_sem, 0, k, 8)
        x = middle_gate(4, recvs[0, k])
        x = top_gate(5, x)
        x = middle_gate(6, x)
        x = top_gate(7, x)
        sends[1, k] = turn(x, mid_t, k)
        start(1, k, "qb", qb, 32)
        return carry

    lax.fori_loop(0, 2, between, 0)

    gate_copies[2].wait()
    gate_copies[3].wait()
    prepare_range(2, 0, 4)
    prepare_range(3, 0, 3)
    prepare(3, 3, None, 1)
    prepare_low(1, 2, low_cos, low_sin)
    row_table(2)
    r, c = iota((256, 256), 0), iota((256, 256), 1)
    one_hot = jnp.where(c == (r % 128) * 2 + r // 128, 1.0, 0.0).astype(BF16)
    co3, si3 = expand(one_hot, row_cos[3:4], row_sin[3:4])
    for b8 in range(2):
        rc, rs = co3[128 * b8 : 128 * b8 + 128], si3[128 * b8 : 128 * b8 + 128]
        for b7 in range(2):
            lc = low_cos[3:4, 128 * b7 : 128 * b7 + 128]
            ls = low_sin[3:4, 128 * b7 : 128 * b7 + 128]
            last_t[b8, b7, 0] = rc * lc - rs * ls
            last_t[b8, b7, 1] = rs * lc + rc * ls

    def arrive1(k, carry):
        finish(recvs, recv_sem, 1, k, 32)
        x = middle_gate(8, recvs[1, k])
        x = top_gate(9, x)
        full[k] = middle_gate(10, x)
        return carry

    lax.fori_loop(0, 2, arrive1, 0)
    a, b = half_swap(full[0], full[1])
    full[0] = a
    full[1] = b

    def leave2(b7, carry):
        x = apply_low(1, b7, full[b7])
        sends[2, b7] = turn(top_gate(11, x), row_t, 2)
        start(2, b7, "qa", qa, 8)
        return carry

    lax.fori_loop(0, 2, leave2, 0)

    for b7 in range(2):
        finish(recvs, recv_sem, 2, b7, 8)
    full_middle(12, recvs.at[2])
    full_top(13)
    full_middle(14, full)
    for b7 in range(2):
        y = dot3(wh[15], wl[15], columns(full[b7]))
        for b8 in range(2):
            re = y[:128, 128 * b8 : 128 * b8 + 128]
            im = y[128:, 128 * b8 : 128 * b8 + 128]
            co, si = last_t[b8, b7, 0], last_t[b8, b7, 1]
            at = 4 * b8 + 2 * b7
            out[pl.ds(at, 128, stride=8), :] = re * co - im * si
            out[pl.ds(at + 1, 128, stride=8), :] = im * co + re * si

    for stage, count in ((0, 8), (1, 32), (2, 8)):
        for k in range(2):
            finish(sends, send_sem, stage, k, count)


def body(amplitudes, gate_blocks, phase_low, phase_high, phase_global):
    cells = amplitudes.shape[1]
    rows = cells // 128
    amp = amplitudes.reshape(2, rows, 128).transpose(1, 0, 2).reshape(2 * rows, 128)
    anywhere = pl.BlockSpec(memory_space=pl.ANY)
    result = pl.pallas_call(
        kernel,
        name="circuit",
        out_shape=pltpu.VMEM((2 * rows, 128), F32),
        in_specs=[anywhere] * 5,
        out_specs=pl.BlockSpec(memory_space=pltpu.VMEM),
        scratch_shapes=[
            pltpu.VMEM((1024, 128), F32),
            pltpu.VMEM((48, 128, 128), F32),
            pltpu.VMEM((4, 256), F32),
            pltpu.VMEM((4, 256), F32),
            pltpu.SMEM((1, 4), F32),
            pltpu.VMEM((3, 256, 256), BF16),
            pltpu.VMEM((16, 256, 256), BF16),
            pltpu.VMEM((16, 256, 256), BF16),
            pltpu.VMEM((2, 2, 256, 256), BF16),
            pltpu.VMEM((2, 2, 256, 128), BF16),
            pltpu.VMEM((2, 512, 128), F32),
            pltpu.VMEM((3, 2, 512, 128), F32),
            pltpu.VMEM((3, 2, 512, 128), F32),
            pltpu.VMEM((3, 2, 512, 128), F32),
            pltpu.VMEM((2, 2, 512, 128), F32),
            pltpu.VMEM((2, 2, 2, 128, 128), F32),
            pltpu.SemaphoreType.DMA((4,)),
            pltpu.SemaphoreType.DMA((4,)),
            pltpu.SemaphoreType.DMA((3, 2)),
            pltpu.SemaphoreType.DMA((3, 2)),
        ],
        compiler_params=pltpu.CompilerParams(
            collective_id=0, has_side_effects=True, vmem_limit_bytes=60 << 20
        ),
    )(amp, gate_blocks.reshape(48, 128, 128), phase_low, phase_high, phase_global.reshape(1, 4))
    return result.reshape(rows, 2, 128).transpose(1, 0, 2).reshape(2, cells)


def solution(mesh):
    return jax.shard_map(
        body,
        mesh=mesh,
        in_specs=(P(None, ("qa", "qb")), P(), P(), P(), P(None, "qa", "qb")),
        out_specs=P(None, ("qa", "qb")),
        check_vma=False,
    )
```

```python
import jax
import jax.numpy as jnp
from jax import lax
from jax.experimental import pallas as pl
from jax.experimental.pallas import tpu as pltpu
from jax.sharding import PartitionSpec as P

F32, BF16 = jnp.float32, jnp.bfloat16
MESH = pl.DeviceIdType.MESH


def dot(a, b):
    return lax.dot_general(a, b, (((1,), (0,)), ((), ())), preferred_element_type=F32)


def dot_t(a, b):
    return lax.dot_general(a, b, (((1,), (1,)), ((), ())), preferred_element_type=F32)


def parts(x):
    high = x.astype(BF16)
    return high, (x - high.astype(F32)).astype(BF16)


def dot3(wh, wl, x):
    xh, xl = parts(x)
    return dot(wh, xh) + dot(wh, xl) + dot(wl, xh)


def iota(shape, axis):
    return lax.broadcasted_iota(jnp.int32, shape, axis)


def half_swap(x, y):
    low = iota(x.shape, 1) < 64
    xr, yr = pltpu.roll(x, 64, 1), pltpu.roll(y, 64, 1)
    return jnp.where(low, x, yr), jnp.where(low, xr, y)


def other_part(x):
    tiles = x.reshape(x.shape[0] // 8, 8, x.shape[1])
    return pltpu.roll(tiles, 4, 1).reshape(x.shape)


def part_sign(shape):
    return jnp.where((iota(shape, 0) // 4) % 2 == 0, -1.0, 1.0).astype(F32)


def embed(re, im):
    return jnp.concatenate(
        [jnp.concatenate([re, -im], axis=1), jnp.concatenate([im, re], axis=1)], axis=0
    )


def kernel(
    amp, gates, p_low, p_high, p_glob, out,
    amp_v, gates_v, low_v, high_v, glob_s, order, wh, wl, bh, bl, full, sends, recvs,
    row_t, mid_t, last_t, in_sem, gate_sem, send_sem, recv_sem,
):
    qa, qb = lax.axis_index("qa"), lax.axis_index("qb")

    gate_copies = [
        pltpu.make_async_copy(
            gates.at[pl.ds(12 * s, 12)], gates_v.at[pl.ds(12 * s, 12)], gate_sem.at[s]
        )
        for s in range(4)
    ]
    amp_copy = pltpu.make_async_copy(amp, amp_v, in_sem.at[0])
    small = [
        pltpu.make_async_copy(p_low, low_v, in_sem.at[1]),
        pltpu.make_async_copy(p_high, high_v, in_sem.at[2]),
        pltpu.make_async_copy(p_glob, glob_s, in_sem.at[3]),
    ]
    gate_copies[0].start()
    amp_copy.start()
    for copy in small:
        copy.start()
    gate_copies[1].start()

    barrier = pltpu.get_barrier_semaphore()

    def greet(axis, me, count):
        def step(i, carry):
            peer = lax.rem(me + i, count)
            pl.semaphore_signal(barrier, inc=1, device_id={axis: peer}, device_id_type=MESH)
            return carry

        lax.fori_loop(1, count, step, 0)

    greet("qa", qa, 8)
    greet("qb", qb, 32)

    p, n = iota((256, 256), 0), iota((256, 256), 1)
    at0 = ((p // 4) % 2) * 128 + ((p // 16) % 8) * 16 + (p % 4) * 4 + ((p // 8) % 2) * 2 + p // 128
    at1 = ((p // 4) % 2) * 128 + (p // 8) * 4 + p % 4
    at2 = (p % 2) * 128 + p // 2
    for i, at in enumerate((at0, at1, at2)):
        order[i] = jnp.where(n == at, 1.0, 0.0).astype(BF16)

    def real_gate(s, g):
        at = (s * 6 + g) * 2
        return embed(gates_v[at], gates_v[at + 1])

    def prepare(s, i, rows, cols):
        h, l = parts(real_gate(s, 1 + i + i // 2))
        if rows is not None:
            both = dot(order[rows], jnp.concatenate([h, l], axis=1)).astype(BF16)
            h, l = both[:, :256], both[:, 256:]
        wh[4 * s + i] = dot_t(h, order[cols]).astype(BF16)
        wl[4 * s + i] = dot_t(l, order[cols]).astype(BF16)

    def prepare_range(s, first, last):
        def step(i, carry):
            prepare(s, i, i % 2, i % 2)
            return carry

        lax.fori_loop(first, last, step, 0)

    def joined_low(s):
        a, b = (s * 6 + 3) * 2, s * 12
        ah, al = parts(embed(gates_v[a], gates_v[a + 1]))
        return dot3(ah, al, jnp.concatenate([gates_v[b], gates_v[b + 1]], axis=0))

    def prepare_low(slot, s, low_cos, low_sin):
        first, second = joined_low(s), joined_low(s + 1)
        re, im = second[:128], second[128:]
        for b7 in range(2):
            co = low_cos[s : s + 1, 128 * b7 : 128 * b7 + 128]
            si = low_sin[s : s + 1, 128 * b7 : 128 * b7 + 128]
            ah, al = parts(embed(re * co - im * si, re * si + im * co))
            h, l = parts(dot3(ah, al, first))
            bh[slot, b7] = jnp.concatenate([h, h], axis=1)
            bl[slot, b7] = l

    def apply_low(slot, b7, x):
        xh, xl = parts(x)
        y = dot_t(jnp.concatenate([xh, xl], axis=1), bh[slot, b7]) + dot_t(xh, bl[slot, b7])
        return y[:, :128] + part_sign((512, 128)) * other_part(y[:, 128:])

    def expand(one_hot, co, si):
        lanes = jnp.concatenate(
            [jnp.broadcast_to(co, (128, 256)), jnp.broadcast_to(si, (128, 256))], axis=0
        )
        h, l = parts(lanes)
        both = dot_t(one_hot, h) + dot_t(one_hot, l)
        return both[:, :128], both[:, 128:]

    def row_one_hot():
        r, c = iota((512, 256), 0), iota((512, 256), 1)
        at = ((r // 16) * 4 + r % 4) * 2 + (r // 8) % 2
        return jnp.where(c == at, 1.0, 0.0).astype(BF16)

    def turn(x, table, at):
        return x * table[at, 0] + other_part(x) * table[at, 1]

    def full_middle(w, src):
        x = jnp.concatenate(
            [
                jnp.concatenate([src[b7, u * 128 : u * 128 + 128] for b7 in range(2)], axis=0)
                for u in range(4)
            ],
            axis=1,
        )
        y = dot3(wh[w], wl[w], x)
        for u in range(4):
            for b7 in range(2):
                full[b7, u * 128 : u * 128 + 128] = y[
                    128 * b7 : 128 * b7 + 128, 128 * u : 128 * u + 128
                ]

    def columns(x):
        x = x.reshape(32, 2, 8, 128)
        return jnp.concatenate([x[:, b8].reshape(256, 128) for b8 in range(2)], axis=1)

    def rows_again(y):
        halves = [y[:, 128 * b8 : 128 * b8 + 128].reshape(32, 1, 8, 128) for b8 in range(2)]
        return jnp.concatenate(halves, axis=1).reshape(512, 128)

    def top_gate(w, x):
        return rows_again(dot3(wh[w], wl[w], columns(x)))

    def full_top(w):
        x = jnp.concatenate([columns(full[b7]) for b7 in range(2)], axis=1)
        y = dot3(wh[w], wl[w], x)
        for b7 in range(2):
            full[b7] = rows_again(y[:, 256 * b7 : 256 * b7 + 256])

    def middle_gate(w, x):
        a, b = half_swap(x[:256], x[256:])
        x = jnp.concatenate(
            [
                jnp.concatenate([a[128 * u : 128 * u + 128], b[128 * u : 128 * u + 128]], axis=0)
                for u in range(2)
            ],
            axis=1,
        )
        y = dot3(wh[w], wl[w], x)
        a = jnp.concatenate([y[:128, :128], y[:128, 128:]], axis=0)
        b = jnp.concatenate([y[128:, :128], y[128:, 128:]], axis=0)
        return jnp.concatenate(half_swap(a, b), axis=0)

    def start(stage, k, axis, me, count):
        size = 512 // count

        def step(i, carry):
            peer = lax.rem(me + i, count) if axis == "qa" else i - 1 + jnp.where(i > me, 1, 0)
            pltpu.make_async_remote_copy(
                src_ref=sends.at[stage, k, pl.ds(pl.multiple_of(peer * size, size), size)],
                dst_ref=recvs.at[stage, k, pl.ds(pl.multiple_of(me * size, size), size)],
                send_sem=send_sem.at[stage, k],
                recv_sem=recv_sem.at[stage, k],
                device_id={axis: peer},
                device_id_type=MESH,
            ).start()
            return carry

        lax.fori_loop(1, count, step, 0)
        own = pl.ds(pl.multiple_of(me * size, size), size)
        recvs[stage, k, own, :] = sends[stage, k, own, :]

    def finish(bufs, sem, stage, k, count):
        moved = 512 - 512 // count
        view = bufs.at[stage, k, pl.ds(0, moved)]
        pltpu.make_async_copy(view, view, sem.at[stage, k]).wait()

    for copy in small:
        copy.wait()
    low_cos, low_sin = jnp.cos(low_v[...]), jnp.sin(low_v[...])
    seg = iota((4, 256), 0)
    glob = jnp.zeros((4, 256), F32)
    for s in range(4):
        glob = jnp.where(seg == s, glob_s[0, s], glob)
    row_cos, row_sin = jnp.cos(high_v[...] + glob), jnp.sin(high_v[...] + glob)

    def row_table(s):
        c, t = expand(row_one_hot(), row_cos[s : s + 1], row_sin[s : s + 1])
        row_t[s, 0] = c
        row_t[s, 1] = part_sign((512, 128)) * t

    row_table(0)
    gate_copies[0].wait()
    amp_copy.wait()
    gate_copies[1].wait()
    gate_copies[2].start()
    gate_copies[3].start()
    prepare(0, 0, 0, 2)
    x = jnp.concatenate([amp_v[256 * u : 256 * u + 256, :] for u in range(4)], axis=1)
    y = dot3(wh[0], wl[0], x)
    for u in range(4):
        for b7 in range(2):
            full[b7, u * 128 : u * 128 + 128] = y[
                128 * b7 : 128 * b7 + 128, 128 * u : 128 * u + 128
            ]
    prepare(0, 1, 1, 1)
    full_top(1)
    prepare(0, 2, 0, 0)
    prepare_low(0, 0, low_cos, low_sin)
    full_middle(2, full)
    prepare(0, 3, 1, 1)
    halves = half_swap(apply_low(0, 0, full[0]), apply_low(0, 1, full[1]))
    y = dot3(wh[3], wl[3], jnp.concatenate([columns(h) for h in halves], axis=1))
    for k in range(2):
        sends[0, k] = turn(rows_again(y[:, 256 * k : 256 * k + 256]), row_t, 0)
    pl.semaphore_wait(barrier, 38)
    for k in range(2):
        start(0, k, "qa", qa, 8)

    prepare_range(1, 0, 4)
    row_table(1)
    v, w = half_swap(
        jnp.broadcast_to(low_cos[1:2, :128], (8, 128)), jnp.broadcast_to(low_cos[1:2, 128:], (8, 128))
    )
    vs, ws = half_swap(
        jnp.broadcast_to(low_sin[1:2, :128], (8, 128)), jnp.broadcast_to(low_sin[1:2, 128:], (8, 128))
    )
    for k, (co, si) in enumerate(((v, vs), (w, ws))):
        co, si = co[:1], si[:1]
        sign = part_sign((512, 128))
        mid_t[k, 0] = row_t[1, 0] * co - row_t[1, 1] * sign * si
        mid_t[k, 1] = row_t[1, 1] * co + row_t[1, 0] * sign * si

    def between(k, carry):
        finish(recvs, recv_sem, 0, k, 8)
        x = middle_gate(4, recvs[0, k])
        x = top_gate(5, x)
        x = middle_gate(6, x)
        x = top_gate(7, x)
        sends[1, k] = turn(x, mid_t, k)
        start(1, k, "qb", qb, 32)
        return carry

    lax.fori_loop(0, 2, between, 0)

    gate_copies[2].wait()
    gate_copies[3].wait()
    prepare_range(2, 0, 4)
    prepare_range(3, 0, 3)
    prepare(3, 3, None, 1)
    prepare_low(1, 2, low_cos, low_sin)
    row_table(2)
    r, c = iota((256, 256), 0), iota((256, 256), 1)
    one_hot = jnp.where(c == (r % 128) * 2 + r // 128, 1.0, 0.0).astype(BF16)
    co3, si3 = expand(one_hot, row_cos[3:4], row_sin[3:4])
    for b8 in range(2):
        rc, rs = co3[128 * b8 : 128 * b8 + 128], si3[128 * b8 : 128 * b8 + 128]
        for b7 in range(2):
            lc = low_cos[3:4, 128 * b7 : 128 * b7 + 128]
            ls = low_sin[3:4, 128 * b7 : 128 * b7 + 128]
            last_t[b8, b7, 0] = rc * lc - rs * ls
            last_t[b8, b7, 1] = rs * lc + rc * ls

    def arrive1(k, carry):
        finish(recvs, recv_sem, 1, k, 32)
        x = middle_gate(8, recvs[1, k])
        x = top_gate(9, x)
        full[k] = turn(top_gate(11, middle_gate(10, x)), row_t, 2)
        return carry

    lax.fori_loop(0, 2, arrive1, 0)
    a, b = half_swap(full[0], full[1])
    full[0] = a
    full[1] = b

    def leave2(b7, carry):
        sends[2, b7] = apply_low(1, b7, full[b7])
        start(2, b7, "qa", qa, 8)
        return carry

    lax.fori_loop(0, 2, leave2, 0)

    for b7 in range(2):
        finish(recvs, recv_sem, 2, b7, 8)
    full_middle(12, recvs.at[2])
    full_top(13)
    full_middle(14, full)
    for b7 in range(2):
        y = dot3(wh[15], wl[15], columns(full[b7]))
        for b8 in range(2):
            re = y[:128, 128 * b8 : 128 * b8 + 128]
            im = y[128:, 128 * b8 : 128 * b8 + 128]
            co, si = last_t[b8, b7, 0], last_t[b8, b7, 1]
            at = 4 * b8 + 2 * b7
            out[pl.ds(at, 128, stride=8), :] = re * co - im * si
            out[pl.ds(at + 1, 128, stride=8), :] = im * co + re * si

    for stage, count in ((0, 8), (1, 32), (2, 8)):
        for k in range(2):
            finish(sends, send_sem, stage, k, count)


def body(amplitudes, gate_blocks, phase_low, phase_high, phase_global):
    cells = amplitudes.shape[1]
    rows = cells // 128
    amp = amplitudes.reshape(2, rows, 128).transpose(1, 0, 2).reshape(2 * rows, 128)
    anywhere = pl.BlockSpec(memory_space=pl.ANY)
    result = pl.pallas_call(
        kernel,
        name="circuit",
        out_shape=pltpu.VMEM((2 * rows, 128), F32),
        in_specs=[anywhere] * 5,
        out_specs=pl.BlockSpec(memory_space=pltpu.VMEM),
        scratch_shapes=[
            pltpu.VMEM((1024, 128), F32),
            pltpu.VMEM((48, 128, 128), F32),
            pltpu.VMEM((4, 256), F32),
            pltpu.VMEM((4, 256), F32),
            pltpu.SMEM((1, 4), F32),
            pltpu.VMEM((3, 256, 256), BF16),
            pltpu.VMEM((16, 256, 256), BF16),
            pltpu.VMEM((16, 256, 256), BF16),
            pltpu.VMEM((2, 2, 256, 256), BF16),
            pltpu.VMEM((2, 2, 256, 128), BF16),
            pltpu.VMEM((2, 512, 128), F32),
            pltpu.VMEM((3, 2, 512, 128), F32),
            pltpu.VMEM((3, 2, 512, 128), F32),
            pltpu.VMEM((3, 2, 512, 128), F32),
            pltpu.VMEM((2, 2, 512, 128), F32),
            pltpu.VMEM((2, 2, 2, 128, 128), F32),
            pltpu.SemaphoreType.DMA((4,)),
            pltpu.SemaphoreType.DMA((4,)),
            pltpu.SemaphoreType.DMA((3, 2)),
            pltpu.SemaphoreType.DMA((3, 2)),
        ],
        compiler_params=pltpu.CompilerParams(
            collective_id=0, has_side_effects=True, vmem_limit_bytes=60 << 20
        ),
    )(amp, gate_blocks.reshape(48, 128, 128), phase_low, phase_high, phase_global.reshape(1, 4))
    return result.reshape(rows, 2, 128).transpose(1, 0, 2).reshape(2, cells)


def solution(mesh):
    return jax.shard_map(
        body,
        mesh=mesh,
        in_specs=(P(None, ("qa", "qb")), P(), P(), P(), P(None, "qa", "qb")),
        out_specs=P(None, ("qa", "qb")),
        check_vma=False,
    )
```

```python
import jax
import jax.numpy as jnp
from jax import lax
from jax.experimental import pallas as pl
from jax.experimental.pallas import tpu as pltpu
from jax.sharding import PartitionSpec as P

F32, BF16 = jnp.float32, jnp.bfloat16
MESH = pl.DeviceIdType.MESH


def dot(a, b):
    return lax.dot_general(a, b, (((1,), (0,)), ((), ())), preferred_element_type=F32)


def dot_t(a, b):
    return lax.dot_general(a, b, (((1,), (1,)), ((), ())), preferred_element_type=F32)


def parts(x):
    high = x.astype(BF16)
    return high, (x - high.astype(F32)).astype(BF16)


def dot3(wh, wl, x):
    xh, xl = parts(x)
    return dot(wh, xh) + dot(wh, xl) + dot(wl, xh)


def iota(shape, axis):
    return lax.broadcasted_iota(jnp.int32, shape, axis)


def half_swap(x, y):
    low = iota(x.shape, 1) < 64
    xr, yr = pltpu.roll(x, 64, 1), pltpu.roll(y, 64, 1)
    return jnp.where(low, x, yr), jnp.where(low, xr, y)


def other_part(x):
    tiles = x.reshape(x.shape[0] // 8, 8, x.shape[1])
    return pltpu.roll(tiles, 4, 1).reshape(x.shape)


def part_sign(shape):
    return jnp.where((iota(shape, 0) // 4) % 2 == 0, -1.0, 1.0).astype(F32)


def embed(re, im):
    return jnp.concatenate(
        [jnp.concatenate([re, -im], axis=1), jnp.concatenate([im, re], axis=1)], axis=0
    )


def kernel(
    amp, gates, p_low, p_high, p_glob, out,
    amp_v, gates_v, low_v, high_v, glob_s, order, wh, wl, bh, bl, full, sends, recvs,
    row_t, mid_t, last_t, in_sem, gate_sem, send_sem, recv_sem,
):
    qa, qb = lax.axis_index("qa"), lax.axis_index("qb")

    gate_copies = [
        pltpu.make_async_copy(gates.at[pl.ds(at, n)], gates_v.at[pl.ds(at, n)], gate_sem.at[i])
        for i, (at, n) in enumerate(((2, 2), (4, 8), (0, 2), (12, 12), (24, 24)))
    ]
    amp_copy = pltpu.make_async_copy(amp, amp_v, in_sem.at[0])
    small = [
        pltpu.make_async_copy(p_low, low_v, in_sem.at[1]),
        pltpu.make_async_copy(p_high, high_v, in_sem.at[2]),
        pltpu.make_async_copy(p_glob, glob_s, in_sem.at[3]),
    ]
    for copy in small + [gate_copies[0], amp_copy] + gate_copies[1:4]:
        copy.start()

    barrier = pltpu.get_barrier_semaphore()

    def greet(axis, me, count):
        def step(i, carry):
            peer = lax.rem(me + i, count)
            pl.semaphore_signal(barrier, inc=1, device_id={axis: peer}, device_id_type=MESH)
            return carry

        lax.fori_loop(1, count, step, 0)

    greet("qa", qa, 8)
    greet("qb", qb, 32)

    p, n = iota((256, 256), 0), iota((256, 256), 1)
    at0 = ((p // 4) % 2) * 128 + ((p // 16) % 8) * 16 + (p % 4) * 4 + ((p // 8) % 2) * 2 + p // 128
    at1 = ((p // 4) % 2) * 128 + (p // 8) * 4 + p % 4
    at2 = (p % 2) * 128 + p // 2
    for i, at in enumerate((at0, at1, at2)):
        order[i] = jnp.where(n == at, 1.0, 0.0).astype(BF16)

    def real_gate(s, g):
        at = (s * 6 + g) * 2
        return embed(gates_v[at], gates_v[at + 1])

    def prepare(s, i, rows, cols):
        h, l = parts(real_gate(s, 1 + i + i // 2))
        if rows is not None:
            both = dot(order[rows], jnp.concatenate([h, l], axis=1)).astype(BF16)
            h, l = both[:, :256], both[:, 256:]
        wh[4 * s + i] = dot_t(h, order[cols]).astype(BF16)
        wl[4 * s + i] = dot_t(l, order[cols]).astype(BF16)

    def prepare_range(s, first, last):
        def step(i, carry):
            prepare(s, i, i % 2, i % 2)
            return carry

        lax.fori_loop(first, last, step, 0)

    def joined_low(s):
        a, b = (s * 6 + 3) * 2, s * 12
        ah, al = parts(embed(gates_v[a], gates_v[a + 1]))
        return dot3(ah, al, jnp.concatenate([gates_v[b], gates_v[b + 1]], axis=0))

    def prepare_low(slot, s, low_cos, low_sin):
        first, second = joined_low(s), joined_low(s + 1)
        re, im = second[:128], second[128:]
        for b7 in range(2):
            co = low_cos[s : s + 1, 128 * b7 : 128 * b7 + 128]
            si = low_sin[s : s + 1, 128 * b7 : 128 * b7 + 128]
            ah, al = parts(embed(re * co - im * si, re * si + im * co))
            h, l = parts(dot3(ah, al, first))
            bh[slot, b7] = jnp.concatenate([h, h], axis=1)
            bl[slot, b7] = l

    def apply_low(slot, b7, x):
        xh, xl = parts(x)
        y = dot_t(jnp.concatenate([xh, xl], axis=1), bh[slot, b7]) + dot_t(xh, bl[slot, b7])
        return y[:, :128] + part_sign((512, 128)) * other_part(y[:, 128:])

    def expand(one_hot, co, si):
        lanes = jnp.concatenate(
            [jnp.broadcast_to(co, (128, 256)), jnp.broadcast_to(si, (128, 256))], axis=0
        )
        h, l = parts(lanes)
        both = dot_t(one_hot, h) + dot_t(one_hot, l)
        return both[:, :128], both[:, 128:]

    def row_one_hot():
        r, c = iota((512, 256), 0), iota((512, 256), 1)
        at = ((r // 16) * 4 + r % 4) * 2 + (r // 8) % 2
        return jnp.where(c == at, 1.0, 0.0).astype(BF16)

    def turn(x, table, at):
        return x * table[at, 0] + other_part(x) * table[at, 1]

    def full_middle(w, src):
        x = jnp.concatenate(
            [
                jnp.concatenate([src[b7, u * 128 : u * 128 + 128] for b7 in range(2)], axis=0)
                for u in range(4)
            ],
            axis=1,
        )
        y = dot3(wh[w], wl[w], x)
        for u in range(4):
            for b7 in range(2):
                full[b7, u * 128 : u * 128 + 128] = y[
                    128 * b7 : 128 * b7 + 128, 128 * u : 128 * u + 128
                ]

    def columns(x):
        x = x.reshape(32, 2, 8, 128)
        return jnp.concatenate([x[:, b8].reshape(256, 128) for b8 in range(2)], axis=1)

    def rows_again(y):
        halves = [y[:, 128 * b8 : 128 * b8 + 128].reshape(32, 1, 8, 128) for b8 in range(2)]
        return jnp.concatenate(halves, axis=1).reshape(512, 128)

    def top_gate(w, x):
        return rows_again(dot3(wh[w], wl[w], columns(x)))

    def full_top(w):
        x = jnp.concatenate([columns(full[b7]) for b7 in range(2)], axis=1)
        y = dot3(wh[w], wl[w], x)
        for b7 in range(2):
            full[b7] = rows_again(y[:, 256 * b7 : 256 * b7 + 256])

    def middle_gate(w, x):
        a, b = half_swap(x[:256], x[256:])
        x = jnp.concatenate(
            [
                jnp.concatenate([a[128 * u : 128 * u + 128], b[128 * u : 128 * u + 128]], axis=0)
                for u in range(2)
            ],
            axis=1,
        )
        y = dot3(wh[w], wl[w], x)
        a = jnp.concatenate([y[:128, :128], y[:128, 128:]], axis=0)
        b = jnp.concatenate([y[128:, :128], y[128:, 128:]], axis=0)
        return jnp.concatenate(half_swap(a, b), axis=0)

    def start(stage, k, axis, me, count):
        size = 512 // count

        def step(i, carry):
            peer = lax.rem(me + i, count) if axis == "qa" else i - 1 + jnp.where(i > me, 1, 0)
            pltpu.make_async_remote_copy(
                src_ref=sends.at[stage, k, pl.ds(pl.multiple_of(peer * size, size), size)],
                dst_ref=recvs.at[stage, k, pl.ds(pl.multiple_of(me * size, size), size)],
                send_sem=send_sem.at[stage, k],
                recv_sem=recv_sem.at[stage, k],
                device_id={axis: peer},
                device_id_type=MESH,
            ).start()
            return carry

        lax.fori_loop(1, count, step, 0)
        own = pl.ds(pl.multiple_of(me * size, size), size)
        recvs[stage, k, own, :] = sends[stage, k, own, :]

    def finish(bufs, sem, stage, k, count):
        moved = 512 - 512 // count
        view = bufs.at[stage, k, pl.ds(0, moved)]
        pltpu.make_async_copy(view, view, sem.at[stage, k]).wait()

    for copy in small:
        copy.wait()
    low_cos, low_sin = jnp.cos(low_v[...]), jnp.sin(low_v[...])
    seg = iota((4, 256), 0)
    glob = jnp.zeros((4, 256), F32)
    for s in range(4):
        glob = jnp.where(seg == s, glob_s[0, s], glob)
    row_cos, row_sin = jnp.cos(high_v[...] + glob), jnp.sin(high_v[...] + glob)

    def row_table(s):
        c, t = expand(row_one_hot(), row_cos[s : s + 1], row_sin[s : s + 1])
        row_t[s, 0] = c
        row_t[s, 1] = part_sign((512, 128)) * t

    row_table(0)
    gate_copies[0].wait()
    amp_copy.wait()
    prepare(0, 0, 0, 2)
    x = jnp.concatenate([amp_v[256 * u : 256 * u + 256, :] for u in range(4)], axis=1)
    y = dot3(wh[0], wl[0], x)
    for u in range(4):
        for b7 in range(2):
            full[b7, u * 128 : u * 128 + 128] = y[
                128 * b7 : 128 * b7 + 128, 128 * u : 128 * u + 128
            ]
    for copy in gate_copies[1:4]:
        copy.wait()
    gate_copies[4].start()
    prepare(0, 1, 1, 1)
    full_top(1)
    prepare(0, 2, 0, 0)
    prepare_low(0, 0, low_cos, low_sin)
    full_middle(2, full)
    prepare(0, 3, 1, 1)
    halves = half_swap(apply_low(0, 0, full[0]), apply_low(0, 1, full[1]))
    y = dot3(wh[3], wl[3], jnp.concatenate([columns(h) for h in halves], axis=1))
    for k in range(2):
        sends[0, k] = turn(rows_again(y[:, 256 * k : 256 * k + 256]), row_t, 0)
    pl.semaphore_wait(barrier, 38)
    for k in range(2):
        start(0, k, "qa", qa, 8)

    prepare_range(1, 0, 4)
    row_table(1)
    v, w = half_swap(
        jnp.broadcast_to(low_cos[1:2, :128], (8, 128)), jnp.broadcast_to(low_cos[1:2, 128:], (8, 128))
    )
    vs, ws = half_swap(
        jnp.broadcast_to(low_sin[1:2, :128], (8, 128)), jnp.broadcast_to(low_sin[1:2, 128:], (8, 128))
    )
    for k, (co, si) in enumerate(((v, vs), (w, ws))):
        co, si = co[:1], si[:1]
        sign = part_sign((512, 128))
        mid_t[k, 0] = row_t[1, 0] * co - row_t[1, 1] * sign * si
        mid_t[k, 1] = row_t[1, 1] * co + row_t[1, 0] * sign * si

    def between(k, carry):
        finish(recvs, recv_sem, 0, k, 8)
        x = middle_gate(4, recvs[0, k])
        x = top_gate(5, x)
        x = middle_gate(6, x)
        x = top_gate(7, x)
        sends[1, k] = turn(x, mid_t, k)
        start(1, k, "qb", qb, 32)
        return carry

    lax.fori_loop(0, 2, between, 0)

    gate_copies[4].wait()
    prepare_range(2, 0, 4)
    prepare_range(3, 0, 3)
    prepare(3, 3, None, 1)
    prepare_low(1, 2, low_cos, low_sin)
    row_table(2)
    r, c = iota((256, 256), 0), iota((256, 256), 1)
    one_hot = jnp.where(c == (r % 128) * 2 + r // 128, 1.0, 0.0).astype(BF16)
    co3, si3 = expand(one_hot, row_cos[3:4], row_sin[3:4])
    for b8 in range(2):
        rc, rs = co3[128 * b8 : 128 * b8 + 128], si3[128 * b8 : 128 * b8 + 128]
        for b7 in range(2):
            lc = low_cos[3:4, 128 * b7 : 128 * b7 + 128]
            ls = low_sin[3:4, 128 * b7 : 128 * b7 + 128]
            last_t[b8, b7, 0] = rc * lc - rs * ls
            last_t[b8, b7, 1] = rs * lc + rc * ls

    def arrive1(k, carry):
        finish(recvs, recv_sem, 1, k, 32)
        x = middle_gate(8, recvs[1, k])
        x = top_gate(9, x)
        full[k] = turn(top_gate(11, middle_gate(10, x)), row_t, 2)
        return carry

    lax.fori_loop(0, 2, arrive1, 0)
    a, b = half_swap(full[0], full[1])
    full[0] = a
    full[1] = b

    def leave2(b7, carry):
        sends[2, b7] = apply_low(1, b7, full[b7])
        start(2, b7, "qa", qa, 8)
        return carry

    lax.fori_loop(0, 2, leave2, 0)

    for b7 in range(2):
        finish(recvs, recv_sem, 2, b7, 8)
    full_middle(12, recvs.at[2])
    full_top(13)
    full_middle(14, full)
    for b7 in range(2):
        y = dot3(wh[15], wl[15], columns(full[b7]))
        for b8 in range(2):
            re = y[:128, 128 * b8 : 128 * b8 + 128]
            im = y[128:, 128 * b8 : 128 * b8 + 128]
            co, si = last_t[b8, b7, 0], last_t[b8, b7, 1]
            at = 4 * b8 + 2 * b7
            out[pl.ds(at, 128, stride=8), :] = re * co - im * si
            out[pl.ds(at + 1, 128, stride=8), :] = im * co + re * si

    for stage, count in ((0, 8), (1, 32), (2, 8)):
        for k in range(2):
            finish(sends, send_sem, stage, k, count)


def body(amplitudes, gate_blocks, phase_low, phase_high, phase_global):
    cells = amplitudes.shape[1]
    rows = cells // 128
    amp = amplitudes.reshape(2, rows, 128).transpose(1, 0, 2).reshape(2 * rows, 128)
    anywhere = pl.BlockSpec(memory_space=pl.ANY)
    result = pl.pallas_call(
        kernel,
        name="circuit",
        out_shape=pltpu.VMEM((2 * rows, 128), F32),
        in_specs=[anywhere] * 5,
        out_specs=pl.BlockSpec(memory_space=pltpu.VMEM),
        scratch_shapes=[
            pltpu.VMEM((1024, 128), F32),
            pltpu.VMEM((48, 128, 128), F32),
            pltpu.VMEM((4, 256), F32),
            pltpu.VMEM((4, 256), F32),
            pltpu.SMEM((1, 4), F32),
            pltpu.VMEM((3, 256, 256), BF16),
            pltpu.VMEM((16, 256, 256), BF16),
            pltpu.VMEM((16, 256, 256), BF16),
            pltpu.VMEM((2, 2, 256, 256), BF16),
            pltpu.VMEM((2, 2, 256, 128), BF16),
            pltpu.VMEM((2, 512, 128), F32),
            pltpu.VMEM((3, 2, 512, 128), F32),
            pltpu.VMEM((3, 2, 512, 128), F32),
            pltpu.VMEM((3, 2, 512, 128), F32),
            pltpu.VMEM((2, 2, 512, 128), F32),
            pltpu.VMEM((2, 2, 2, 128, 128), F32),
            pltpu.SemaphoreType.DMA((4,)),
            pltpu.SemaphoreType.DMA((5,)),
            pltpu.SemaphoreType.DMA((3, 2)),
            pltpu.SemaphoreType.DMA((3, 2)),
        ],
        compiler_params=pltpu.CompilerParams(
            collective_id=0, has_side_effects=True, vmem_limit_bytes=60 << 20
        ),
    )(amp, gate_blocks.reshape(48, 128, 128), phase_low, phase_high, phase_global.reshape(1, 4))
    return result.reshape(rows, 2, 128).transpose(1, 0, 2).reshape(2, cells)


def solution(mesh):
    return jax.shard_map(
        body,
        mesh=mesh,
        in_specs=(P(None, ("qa", "qb")), P(), P(), P(), P(None, "qa", "qb")),
        out_specs=P(None, ("qa", "qb")),
        check_vma=False,
    )
```
